32 devices in a mesh: dp: 8 (over y, x, core), mp: 4 (over z).
Axes of the slice: x: 2, y: 2, z: 4, core: 2. Of those that a mesh axis runs over, the one named last changes fastest.
Arguments:
- page_pool: bfloat16 [512, 128, 512], P('dp'), may hold values from -6 to 6
- move_count: int32 [8, 8], P('dp'), may hold values from 0 to 2, as said below
- send_slots: int32 [64, 2], P('dp'), may hold values from 0 to 63, as said below
- page_table: int32 [512, 16], P('dp'), may hold values from 0 to 79, as said below
- history_len: int32 [512], P('dp'), may hold values from 1 to 2048, as said below
- queries: bfloat16 [512, 8, 256], P('dp', 'mp'), may hold values from -6 to 6
- new_entry: bfloat16 [512, 512], P('dp'), may hold values from -6 to 6
- residual: bfloat16 [512, 2048], P('dp'), may hold values from -30 to 30
- out_proj: bfloat16 [2048, 2048], P('mp'), may hold values from -0.125 to 0.125
- ffn_gain: float32 [2048], replicated, may hold values from -0.5 to 0.5
- gate_proj: bfloat16 [2048, 16384], P(None, ('dp', 'mp')), may hold values from -0.125 to 0.125
- up_proj: bfloat16 [2048, 16384], P(None, ('dp', 'mp')), may hold values from -0.125 to 0.125
- down_proj: bfloat16 [16384, 2048], P(('dp', 'mp')), may hold values from -0.046875 to 0.046875
Outputs:
- arrived: bfloat16 [128, 128, 512], P('dp')
- layer_out: bfloat16 [512, 2048], P('dp')
The draws below stay inside these ranges and needn't reach their ends.
Inputs may be any that keep to these rules, and one draw needn't show every extreme that they name: `move_count`: zero on the diagonal; in every draw one device receives exactly 2 pages from every other device. `send_slots`: only the first move_count[s, d] entries of row s * 8 + d are sent. `page_table`: for a game of device d, an entry e >= 64 equals 64 + s * 2 + c with c < move_count[s, d]. `history_len`: some game of some device reaches 2048 in every draw.
All inputs are finite; a program needn't handle non-finite values.
Results may differ from the reference program's by a relative error of at most 0.0075.
Values may be sent and summed in bfloat16 or wider, within the bound.
A program may use at most 128 MiB of HBM per device.

```python
import math
import jax
import jax.numpy as jnp
from jax import lax

D = 2048
HEADS = 8
HD = 256
FF = 16384
PAGE = 128
MAXP = 16
CAP = 2
GAMES_DEV = 64
POOL = 64
POOL_ALL = 512
GAMES = 512
N_DP = 8


def plan_counts(key):
    base = jax.random.fold_in(key, 11)
    first, second = jax.random.split(base)
    counts = jax.random.randint(first, (N_DP, N_DP), 0, CAP + 1)
    busiest = jax.random.randint(second, (), 0, N_DP)
    places = jnp.arange(N_DP)
    counts = jnp.where(places[None, :] == busiest, CAP, counts)
    counts = jnp.where(places[:, None] == places[None, :], 0, counts)
    return counts.astype(jnp.int32)


def draw_move_count(key, part):
    return plan_counts(key)


def draw_send_slots(key, part):
    return jax.random.randint(jax.random.fold_in(key, 12), (N_DP * N_DP, CAP), 0, POOL).astype(jnp.int32)


def draw_page_table(key, part):
    counts = plan_counts(key)
    first, second = jax.random.split(jax.random.fold_in(key, 13))
    picks = jax.random.randint(first, (GAMES, MAXP), 0, POOL + N_DP * CAP)
    resident = jax.random.randint(second, (GAMES, MAXP), 0, POOL)
    owner = (jnp.arange(GAMES) // GAMES_DEV)[:, None]
    source = jnp.clip((picks - POOL) // CAP, 0, N_DP - 1)
    column = (picks - POOL) % CAP
    usable = (picks >= POOL) & (column < counts[source, owner])
    table = jnp.where(picks < POOL, picks, jnp.where(usable, picks, resident))
    return table.astype(jnp.int32)


def draw_history_len(key, part):
    first, second, third = jax.random.split(jax.random.fold_in(key, 14), 3)
    longest = MAXP * PAGE
    levels = longest.bit_length() - 1
    powers = jax.random.randint(first, (GAMES,), 0, levels + 1)
    ceiling = jnp.minimum(jnp.left_shift(jnp.ones((GAMES,), jnp.int32), powers.astype(jnp.int32)), longest)
    lengths = jax.random.randint(second, (GAMES,), 1, ceiling + 1)
    chosen = jax.random.randint(third, (), 0, GAMES)
    lengths = jnp.where(jnp.arange(GAMES) == chosen, longest, lengths)
    return lengths.astype(jnp.int32)


def draw_page_pool(key, part):
    noise = jax.random.fold_in(key, 31)
    shape = (POOL_ALL, PAGE, 2 * HD)
    values = jax.random.truncated_normal(noise, -6.0, 6.0, shape, jnp.float32)
    return values.astype(jnp.bfloat16)


def draw_queries(key, part):
    first = jax.random.fold_in(jax.random.fold_in(key, 41), 0)
    shape = (GAMES, HEADS, HD)
    values = jax.random.truncated_normal(first, -6.0, 6.0, shape, jnp.float32)
    return values.astype(jnp.bfloat16)


def draw_residual(key, part):
    first = jax.random.fold_in(jax.random.fold_in(key, 51), 0)
    values = jax.random.truncated_normal(first, -6.0, 6.0, (GAMES, D), jnp.float32)
    return values.astype(jnp.bfloat16)


def steps_of(own_key, extent, pieces, low, top_value):
    gain = 1.0
    for axis_at, parts in pieces:
        steps = jax.random.uniform(jax.random.fold_in(jax.random.fold_in(own_key, 6), axis_at), (parts,), jnp.float32, low / len(pieces), top_value / len(pieces))
        gain = gain * jnp.repeat(jnp.exp(steps), extent[axis_at] // parts).reshape((-1,) + (1,) * (len(extent) - 1 - axis_at))
    return gain


def centred(stream_key, extent, scale, bound, cuts=(), kind=jnp.bfloat16):
    entries = jax.random.normal(stream_key, extent, jnp.float32) * scale
    if len(cuts) > 0:
        entries = steps_of(stream_key, extent, cuts, -0.22, 0.18) * entries
    return jnp.clip(entries, min=-bound, max=bound).astype(kind)


def setup_inputs(seed: int = 0) -> dict:
    key_list = jax.random.split(jax.random.key(seed), 14)
    page_pool = draw_page_pool(jax.random.fold_in(key_list[13], 71), 0)
    move_count = draw_move_count(jax.random.fold_in(key_list[13], 71), 0)
    send_slots = draw_send_slots(jax.random.fold_in(key_list[13], 71), 0)
    page_table = draw_page_table(jax.random.fold_in(key_list[13], 71), 0)
    history_len = draw_history_len(jax.random.fold_in(key_list[13], 71), 0)
    queries = draw_queries(jax.random.fold_in(key_list[13], 71), 0)
    new_entry = centred(key_list[6], (GAMES, 2 * HD), 1.0, 6.0, ((0, 8),))
    residual = draw_residual(jax.random.fold_in(key_list[13], 71), 0)
    out_proj = centred(key_list[8], (HEADS * HD, D), (HEADS * HD) ** -0.5, 0.125, ((0, 4),))
    ffn_gain = jnp.clip(jax.random.uniform(key_list[9], (D,), jnp.float32, -0.5, 0.5), -0.5, 0.5)
    gate_proj = centred(key_list[10], (D, FF), D ** -0.5, 0.125, ((1, 32),))
    up_proj = centred(key_list[11], (D, FF), D ** -0.5, 0.125, ((1, 32),))
    down_proj = centred(key_list[12], (FF, D), FF ** -0.5, 0.046875, ((0, 32),))
    return dict(page_pool=page_pool, move_count=move_count, send_slots=send_slots, page_table=page_table, history_len=history_len, queries=queries, new_entry=new_entry, residual=residual, out_proj=out_proj, ffn_gain=ffn_gain, gate_proj=gate_proj, up_proj=up_proj, down_proj=down_proj)


def attend_block(query_blk, page_rows, length_blk, entry_blk):
    keys = page_rows[:, :, :HD].astype(jnp.float32)
    values = page_rows[:, :, HD:].astype(jnp.float32)
    query_f = query_blk.astype(jnp.float32)
    entry_f = entry_blk.astype(jnp.float32)
    factor = 1.0 / math.sqrt(HD)
    scores = jnp.einsum('bhd,btd->bht', query_f, keys) * factor
    own = jnp.einsum('bhd,bd->bh', query_f, entry_f[:, :HD]) * factor
    places = jnp.arange(page_rows.shape[1], dtype=jnp.int32)
    valid = places[None, None, :] < length_blk[:, None, None]
    scores = jnp.where(valid, scores, jnp.float32(-1e+30))
    biggest = jnp.maximum(lax.optimization_barrier(jnp.max(scores, axis=-1)), own)
    probs = jnp.where(valid, jnp.exp(scores - biggest[..., None]), jnp.float32(0.0))
    prob_own = jnp.exp(own - biggest)
    denom = lax.optimization_barrier(jnp.sum(probs, axis=-1)) + prob_own
    weights = (probs / denom[..., None]).astype(jnp.bfloat16)
    weight_own = (prob_own / denom).astype(jnp.bfloat16)
    weights = lax.optimization_barrier(weights).astype(jnp.float32)
    weight_own = lax.optimization_barrier(weight_own).astype(jnp.float32)
    result = jnp.einsum('bht,btd->bhd', weights, values)
    result = result + weight_own[..., None] * entry_f[:, None, HD:]
    return result.astype(jnp.bfloat16)

def reference(page_pool, move_count, send_slots, page_table, history_len, queries, new_entry, residual, out_proj, ffn_gain, gate_proj, up_proj, down_proj):
    slots = send_slots.reshape(N_DP, N_DP, CAP)
    owners = jnp.arange(N_DP, dtype=jnp.int32)[:, None, None] * POOL + slots.astype(jnp.int32)
    live = jnp.arange(CAP, dtype=jnp.int32)[None, None, :] < move_count[:, :, None]
    owners = jnp.transpose(owners, (1, 0, 2)).reshape(-1)
    live = jnp.transpose(live, (1, 0, 2)).reshape(-1)
    arrived = jnp.where(live[:, None, None], page_pool[owners], jnp.zeros((), jnp.bfloat16))
    block = math.gcd(GAMES_DEV, 8)

    def one_device(index):
        own_pages = lax.dynamic_slice_in_dim(page_pool, (index * POOL).astype(jnp.int32), POOL, 0)
        got_pages = lax.dynamic_slice_in_dim(arrived, (index * N_DP * CAP).astype(jnp.int32), N_DP * CAP, 0)
        every_page = jnp.concatenate([own_pages, got_pages], axis=0)
        first = (index * GAMES_DEV).astype(jnp.int32)
        table = lax.dynamic_slice_in_dim(page_table, first, GAMES_DEV, 0).reshape(-1, block, MAXP)
        lengths = lax.dynamic_slice_in_dim(history_len, first, GAMES_DEV, 0).reshape(-1, block)
        query_dev = lax.dynamic_slice_in_dim(queries, first, GAMES_DEV, 0).reshape(-1, block, HEADS, HD)
        entry_dev = lax.dynamic_slice_in_dim(new_entry, first, GAMES_DEV, 0).reshape(-1, block, 2 * HD)

        def one_block(items):
            table_blk, length_blk, query_blk, entry_blk = items
            page_rows = every_page[table_blk].reshape(block, MAXP * PAGE, 2 * HD)
            return attend_block(query_blk, page_rows, length_blk, entry_blk)
        result = lax.map(one_block, (table, lengths, query_dev, entry_dev))
        return result.reshape(GAMES_DEV, HEADS * HD)
    attended = lax.map(one_device, jnp.arange(N_DP, dtype=jnp.int32)).reshape(GAMES, HEADS * HD)
    stream_in = residual.astype(jnp.float32) + jnp.dot(attended, out_proj, preferred_element_type=jnp.float32)
    scale_row = lax.rsqrt(lax.optimization_barrier(jnp.mean(stream_in * stream_in, axis=-1, keepdims=True)) + 1e-06)
    normed = (stream_in * scale_row * (1.0 + ffn_gain)).astype(jnp.bfloat16)
    gate = jnp.dot(normed, gate_proj, preferred_element_type=jnp.float32)
    up_val = jnp.dot(normed, up_proj, preferred_element_type=jnp.float32)
    hidden = (jax.nn.gelu(gate, approximate=True) * up_val).astype(jnp.bfloat16)
    mixed = jnp.dot(hidden, down_proj, preferred_element_type=jnp.float32)
    layer_out = (stream_in + mixed).astype(jnp.bfloat16)
    return (arrived, layer_out)
```

```python
import functools
import math

import jax
import jax.numpy as jnp
from jax import lax
from jax.experimental import pallas as pl
from jax.experimental.pallas import tpu as pltpu
from jax.sharding import PartitionSpec as P

F32 = jnp.float32
BF16 = jnp.bfloat16


def remote(src, dst, send, recv, axis, peer):
    return pltpu.make_async_remote_copy(
        src_ref=src,
        dst_ref=dst,
        send_sem=send,
        recv_sem=recv,
        device_id={axis: peer},
        device_id_type=pl.DeviceIdType.MESH,
    )


def flip(index, bit):
    size = 1 << bit
    return index + size * (1 - 2 * ((index // size) % 2))


def flips(index, bits):
    found = [index]
    for bit in bits:
        found = found + [flip(f, bit) for f in found]
    return found


def with_bits(index, bits, number):
    for place, bit in enumerate(bits):
        size = 1 << bit
        index = index + size * (((number >> place) & 1) - (index // size) % 2)
    return index


def dot(a, b):
    return jnp.dot(a, b, preferred_element_type=F32)


def step(
    n_dp,
    n_mp,
    count_ref,
    slot_ref,
    table_ref,
    length_ref,
    query_ref,
    entry_ref,
    residual_ref,
    gain_ref,
    pool_hbm,
    wo_hbm,
    wg_hbm,
    wu_hbm,
    wd_hbm,
    arrived_hbm,
    out_ref,
    pages,
    landed,
    outgoing,
    wo,
    wg,
    wu,
    wd,
    head32,
    head16,
    sums16,
    head_got,
    sums_got,
    feats,
    hidden,
    part,
    got,
    pool_sem,
    weight_sem,
    arrived_sem,
    page_send,
    page_recv,
    z_send,
    z_recv,
    ag_send,
    ag_recv,
    rs_send,
    rs_recv,
):
    dp = lax.axis_index("dp")
    mp = lax.axis_index("mp")
    bits = n_dp.bit_length() - 1
    pool, page_len, width = pool_hbm.shape
    cap = slot_ref.shape[1]
    games, table_len = table_ref.shape
    rows, head_size = query_ref.shape
    heads = rows // games
    model = residual_ref.shape[1]
    half = model // 2
    share = games // n_mp
    every = pool + n_dp * cap
    group = math.gcd(pool, n_dp * cap, 8)
    pool_loads = []
    for at in range(0, pool, group):
        copy = pltpu.make_async_copy(
            pool_hbm.at[pl.ds(at, group)], pages.at[pl.ds(at, group)], pool_sem.at[at // group]
        )
        copy.start()
        pool_loads.append(copy)
    weight_loads = []
    for i, (src, dst) in enumerate(((wo_hbm, wo), (wg_hbm, wg), (wu_hbm, wu), (wd_hbm, wd))):
        copy = pltpu.make_async_copy(src, dst, weight_sem.at[i])
        copy.start()
        weight_loads.append(copy)

    barrier = pltpu.get_barrier_semaphore()
    for axis, n, me in (("dp", n_dp, dp), ("mp", n_mp, mp)):
        for o in range(1, n):
            pl.semaphore_signal(
                barrier,
                inc=1,
                device_id={axis: lax.rem(me + o, n)},
                device_id_type=pl.DeviceIdType.MESH,
            )
    for copy in pool_loads:
        copy.wait()
    for d in range(n_dp):
        for c in range(cap):
            page = pages[slot_ref[d, c]]
            live = jnp.full(page.shape, c < count_ref[0, d])
            outgoing[d * cap + c] = jnp.where(live, page, jnp.zeros_like(page))
    pl.semaphore_wait(barrier, n_dp - 1 + n_mp - 1)

    sends = []
    for o in range(1, n_dp):
        to = lax.rem(dp + o, n_dp)
        copy = remote(
            outgoing.at[pl.ds(to * cap, cap)],
            landed.at[pl.ds(dp * cap, cap)],
            page_send.at[o - 1],
            page_recv.at[o - 1],
            "dp",
            to,
        )
        copy.start()
        sends.append(copy)
    landed[pl.ds(dp * cap, cap)] = outgoing[pl.ds(dp * cap, cap)]

    table = table_ref[...]
    length = length_ref[...]
    whole_pages = lax.div(length, jnp.int32(page_len))
    rest = length - whole_pages * page_len
    lane = lax.broadcasted_iota(jnp.int32, (games, every), 1)
    full = jnp.zeros((games, every), F32)
    last = jnp.full((games, 1), -1, jnp.int32)
    for j in range(table_len):
        named = table[:, j : j + 1]
        full = full + jnp.where((lane == named) & (whole_pages > j), 1.0, 0.0)
        last = jnp.where(whole_pages == j, named, last)
    full = jnp.concatenate([full] * heads, axis=0)
    last = jnp.concatenate([last] * heads, axis=0)
    rest = jnp.concatenate([rest] * heads, axis=0)
    place = lax.broadcasted_iota(jnp.int32, (rows, page_len), 1)
    in_last = jnp.where(place < rest, 1.0, 0.0)

    factor = 1.0 / math.sqrt(head_size)
    query = query_ref[...]
    entry = entry_ref[...].astype(F32)
    entry = jnp.concatenate([entry] * heads, axis=0)
    biggest = (
        jnp.sum(query.astype(F32) * entry[:, :head_size], axis=-1, keepdims=True) * factor
    )
    total = jnp.ones((rows, 1), F32)
    acc = entry[:, head_size:]

    def attend(at, state):
        biggest, total, acc = state
        block = pages.at[pl.ds(at, group)] if at < pool else landed.at[pl.ds(at - pool, group)]
        keys = block[:, :, :head_size].reshape(group * page_len, head_size)
        values = block[:, :, head_size:].reshape(group * page_len, head_size)
        scores = (
            lax.dot_general(query, keys, (((1,), (1,)), ((), ())), preferred_element_type=F32)
            * factor
        )
        times = jnp.concatenate(
            [
                full[:, e : e + 1] + jnp.where(last == e, in_last, 0.0)
                for e in range(at, at + group)
            ],
            axis=1,
        )
        scores = jnp.where(times > 0.0, scores, -1e30)
        new = jnp.maximum(biggest, jnp.max(scores, axis=-1, keepdims=True))
        probs = times * jnp.exp(scores - new)
        shrink = jnp.exp(biggest - new)
        total = total * shrink + jnp.sum(probs, axis=-1, keepdims=True)
        acc = acc * shrink + dot(probs.astype(BF16), values)
        return new, total, acc

    state = (biggest, total, acc)
    for at in range(0, pool, group):
        state = attend(at, state)
    for o in range(1, n_dp):
        source = lax.rem(dp - o + n_dp, n_dp)
        slot = landed.at[pl.ds(source * cap, cap)]
        remote(slot, slot, page_send.at[o - 1], page_recv.at[o - 1], "dp", source).wait_recv()
    arrived_copy = pltpu.make_async_copy(landed, arrived_hbm, arrived_sem)
    arrived_copy.start()
    for at in range(pool, every, group):
        state = attend(at, state)
    biggest, total, acc = state
    attended = (acc / total).astype(BF16)
    attended = jnp.concatenate(
        [attended[h * games : (h + 1) * games] for h in range(heads)], axis=1
    )
    weight_loads[0].wait()
    head = dot(attended, wo[...])
    head32[...] = head
    head16[...] = head.astype(BF16)

    def sum_mp(block, landing, base):
        for o in range(1, n_mp):
            to = lax.rem(mp + o, n_mp)
            copy = remote(
                block.at[pl.ds(pl.multiple_of(to * share, share), share)],
                landing.at[o - 1],
                z_send.at[base + o - 1],
                z_recv.at[base + o - 1],
                "mp",
                to,
            )
            copy.start()
            sends.append(copy)
        total = head32[pl.ds(pl.multiple_of(mp * share, share), share)]
        for o in range(1, n_mp):
            remote(
                landing.at[o - 1],
                landing.at[o - 1],
                z_send.at[base + o - 1],
                z_recv.at[base + o - 1],
                "mp",
                lax.rem(mp - o + n_mp, n_mp),
            ).wait_recv()
            total = total + landing[o - 1].astype(F32)
        return total

    def spread_mp(views, base):
        per = len(views(mp))
        for o in range(1, n_mp):
            for i, view in enumerate(views(mp)):
                sem = base + (o - 1) * per + i
                copy = remote(
                    view, view, z_send.at[sem], z_recv.at[sem], "mp", lax.rem(mp + o, n_mp)
                )
                copy.start()
                sends.append(copy)
        for o in range(1, n_mp):
            source = lax.rem(mp - o + n_mp, n_mp)
            for i, view in enumerate(views(source)):
                sem = base + (o - 1) * per + i
                remote(view, view, z_send.at[sem], z_recv.at[sem], "mp", source).wait_recv()

    def own_rows(m):
        return pl.ds(pl.multiple_of(m * share, share), share)

    peers = n_mp - 1
    mine = residual_ref[own_rows(mp)].astype(F32) + sum_mp(head16, head_got, 0)
    scale = lax.rsqrt(jnp.mean(mine * mine, axis=-1, keepdims=True) + 1e-6)
    normed = (mine * scale * (1.0 + gain_ref[...])).astype(BF16)
    for k in range(2):
        feats[k, dp, own_rows(mp)] = normed[:, k * half : (k + 1) * half]
    spread_mp(lambda m: [feats.at[k, dp, own_rows(m)] for k in range(2)], peers)

    orders = [list(range(1, bits)) + [0], list(range(2, bits)) + [1, 0] if bits > 1 else [0]]
    for t in range(bits):
        waits = []
        for k in range(2):
            bit = orders[k][t]
            peer = flip(dp, bit)
            held = flips(dp, orders[k][:t])
            for i, block in enumerate(held):
                sem = (1 << t) - 1 + i
                copy = remote(
                    feats.at[k, block],
                    feats.at[k, block],
                    ag_send.at[k, sem],
                    ag_recv.at[k, sem],
                    "dp",
                    peer,
                )
                copy.start()
                sends.append(copy)
                other = flip(block, bit)
                waits.append(
                    remote(
                        feats.at[k, other],
                        feats.at[k, other],
                        ag_send.at[k, sem],
                        ag_recv.at[k, sem],
                        "dp",
                        peer,
                    )
                )
        for wait in waits:
            wait.wait_recv()

    for copy in weight_loads[1:]:
        copy.wait()
    all_games = n_dp * games
    units = wg.shape[1]
    tile = math.gcd(units, 256)

    @pl.loop(0, units // tile)
    def _(i):
        columns = pl.ds(pl.multiple_of(i * tile, tile), tile)
        low = feats[0].reshape(all_games, half)
        high = feats[1].reshape(all_games, half)
        gate = dot(low, wg[:half, columns]) + dot(high, wg[half:, columns])
        up = dot(low, wu[:half, columns]) + dot(high, wu[half:, columns])
        bent = jnp.tanh(math.sqrt(2.0 / math.pi) * (gate + 0.044715 * (gate * gate * gate)))
        hidden[:, columns] = (0.5 * gate * (1.0 + bent) * up).astype(BF16)

    def halving(k, t):
        order = orders[k][::-1]
        bit, after = order[t], order[t + 1 :]
        base = sum(1 << (bits - 1 - s) for s in range(t))
        peer = flip(dp, bit)
        waits = []
        for i in range(1 << len(after)):
            keep = with_bits(dp, after, i)
            copy = remote(
                part.at[k, flip(keep, bit)],
                got.at[k, base + i],
                rs_send.at[k, base + i],
                rs_recv.at[k, base + i],
                "dp",
                peer,
            )
            copy.start()
            sends.append(copy)
            waits.append((copy, keep, base + i))
        return waits

    out_tile = math.gcd(half, 512)
    waiting = []
    for k in range(2):

        @pl.loop(0, half // out_tile)
        def _(i):
            columns = pl.ds(pl.multiple_of(k * half + i * out_tile, out_tile), out_tile)
            inner = pl.ds(pl.multiple_of(i * out_tile, out_tile), out_tile)
            block = dot(hidden[...], wd[:, columns]).astype(BF16)
            part[k, :, :, inner] = block.reshape(n_dp, games, out_tile)

        waiting.append(halving(k, 0))
    for t in range(bits):
        later = []
        for k in range(2):
            for copy, keep, slot in waiting[k]:
                copy.wait_recv()
                added = part[k, keep].astype(F32) + got[k, slot].astype(F32)
                if t == bits - 1:
                    head32[:, k * half : (k + 1) * half] = added
                    sums16[:, k * half : (k + 1) * half] = added.astype(BF16)
                else:
                    part[k, keep] = added.astype(BF16)
            if t < bits - 1:
                later.append(halving(k, t + 1))
        waiting = later

    mixed = sum_mp(sums16, sums_got, 3 * peers)
    out_ref[own_rows(mp)] = (mine + mixed).astype(BF16)
    spread_mp(lambda m: [out_ref.at[own_rows(m)]], 4 * peers)
    for copy in sends:
        copy.wait_send()
    arrived_copy.wait()


def local(
    page_pool,
    move_count,
    send_slots,
    page_table,
    history_len,
    queries,
    new_entry,
    residual,
    out_proj,
    ffn_gain,
    gate_proj,
    up_proj,
    down_proj,
):
    n_dp = lax.axis_size("dp")
    n_mp = lax.axis_size("mp")
    pool, page_len, width = page_pool.shape
    cap = send_slots.shape[1]
    games, heads, head_size = queries.shape
    model = residual.shape[1]
    units = gate_proj.shape[1]
    half = model // 2
    share = games // n_mp
    group = math.gcd(pool, n_dp * cap, 8)
    query_rows = jnp.transpose(queries, (1, 0, 2)).reshape(heads * games, head_size)
    vmem = pl.BlockSpec(memory_space=pltpu.VMEM)
    smem = pl.BlockSpec(memory_space=pltpu.SMEM)
    hbm = pl.BlockSpec(memory_space=pl.ANY)
    dma = pltpu.SemaphoreType.DMA
    z_count = 5 * (n_mp - 1)
    return pl.pallas_call(
        functools.partial(step, n_dp, n_mp),
        out_shape=(
            jax.ShapeDtypeStruct((n_dp * cap, page_len, width), BF16),
            jax.ShapeDtypeStruct((games, model), BF16),
        ),
        in_specs=[smem, smem] + [vmem] * 6 + [hbm] * 5,
        out_specs=(hbm, vmem),
        scratch_shapes=[
            pltpu.VMEM((pool, page_len, width), BF16),
            pltpu.VMEM((n_dp * cap, page_len, width), BF16),
            pltpu.VMEM((n_dp * cap, page_len, width), BF16),
            pltpu.VMEM(out_proj.shape, BF16),
            pltpu.VMEM(gate_proj.shape, BF16),
            pltpu.VMEM(up_proj.shape, BF16),
            pltpu.VMEM(down_proj.shape, BF16),
            pltpu.VMEM((games, model), F32),
            pltpu.VMEM((games, model), BF16),
            pltpu.VMEM((games, model), BF16),
            pltpu.VMEM((n_mp - 1, share, model), BF16),
            pltpu.VMEM((n_mp - 1, share, model), BF16),
            pltpu.VMEM((2, n_dp, games, half), BF16),
            pltpu.VMEM((n_dp * games, units), BF16),
            pltpu.VMEM((2, n_dp, games, half), BF16),
            pltpu.VMEM((2, n_dp - 1, games, half), BF16),
            dma((pool // group,)),
            dma((4,)),
            dma,
            dma((n_dp - 1,)),
            dma((n_dp - 1,)),
            dma((z_count,)),
            dma((z_count,)),
            dma((2, n_dp - 1)),
            dma((2, n_dp - 1)),
            dma((2, n_dp - 1)),
            dma((2, n_dp - 1)),
        ],
        compiler_params=pltpu.CompilerParams(
            collective_id=0, has_side_effects=True, vmem_limit_bytes=63 * 1024 * 1024
        ),
        cost_estimate=pl.CostEstimate(
            flops=6 * n_dp * games * model * units,
            bytes_accessed=2 * (page_pool.size + 4 * model * units),
            transcendentals=n_dp * games * units,
        ),
    )(
        move_count,
        send_slots,
        page_table,
        history_len.reshape(games, 1),
        query_rows,
        new_entry,
        residual,
        ffn_gain.reshape(1, model),
        page_pool,
        out_proj,
        gate_proj,
        up_proj,
        down_proj,
    )


def solution(mesh):
    in_specs = (
        P("dp", None, None),
        P("dp", None),
        P("dp", None),
        P("dp", None),
        P("dp"),
        P("dp", "mp", None),
        P("dp", None),
        P("dp", None),
        P("mp", None),
        P(),
        P(None, ("dp", "mp")),
        P(None, ("dp", "mp")),
        P(("dp", "mp"), None),
    )
    out_specs = (P("dp", None, None), P("dp", None))
    return jax.shard_map(local, mesh=mesh, in_specs=in_specs, out_specs=out_specs, check_vma=False)
```

```python
import functools
import math

import jax
import jax.numpy as jnp
from jax import lax
from jax.experimental import pallas as pl
from jax.experimental.pallas import tpu as pltpu
from jax.sharding import PartitionSpec as P

F32 = jnp.float32
BF16 = jnp.bfloat16


def remote(src, dst, send, recv, axis, peer):
    return pltpu.make_async_remote_copy(
        src_ref=src,
        dst_ref=dst,
        send_sem=send,
        recv_sem=recv,
        device_id={axis: peer},
        device_id_type=pl.DeviceIdType.MESH,
    )


def flip(index, bit):
    size = 1 << bit
    return index + size * (1 - 2 * ((index // size) % 2))


def flips(index, bits):
    found = [index]
    for bit in bits:
        found = found + [flip(f, bit) for f in found]
    return found


def xor(index, number):
    for bit in range(number.bit_length()):
        if (number >> bit) & 1:
            index = flip(index, bit)
    return index


def with_bits(index, bits, number):
    for place, bit in enumerate(bits):
        size = 1 << bit
        index = index + size * (((number >> place) & 1) - (index // size) % 2)
    return index


def dot(a, b):
    return jnp.dot(a, b, preferred_element_type=F32)


def step(
    n_dp,
    n_mp,
    count_ref,
    slot_ref,
    table_ref,
    length_ref,
    query_ref,
    entry_ref,
    residual_ref,
    gain_ref,
    pool_hbm,
    wo_hbm,
    wg_hbm,
    wu_hbm,
    wd_hbm,
    arrived_hbm,
    out_ref,
    pages,
    landed,
    outgoing,
    wo,
    wg,
    wu,
    wd,
    head32,
    head16,
    sums16,
    head_got,
    sums_got,
    feats,
    hidden,
    part,
    got,
    pool_sem,
    weight_sem,
    arrived_sem,
    page_send,
    page_recv,
    z_send,
    z_recv,
    ag_send,
    ag_recv,
    rs_send,
    rs_recv,
):
    dp = lax.axis_index("dp")
    mp = lax.axis_index("mp")
    bits = n_dp.bit_length() - 1
    pool, page_len, width = pool_hbm.shape
    cap = slot_ref.shape[0]
    table_len, games = table_ref.shape
    _, heads, head_size = query_ref.shape
    rows = heads * games
    model = residual_ref.shape[1]
    half = model // 2
    share = games // n_mp
    every = pool + n_dp * cap
    group = math.gcd(pool, n_dp * cap, 8)
    pool_loads = []
    for at in range(0, pool, group):
        copy = pltpu.make_async_copy(
            pool_hbm.at[pl.ds(at, group)], pages.at[pl.ds(at, group)], pool_sem.at[at // group]
        )
        copy.start()
        pool_loads.append(copy)
    barrier = pltpu.get_barrier_semaphore()
    for axis, n, me in (("dp", n_dp, dp), ("mp", n_mp, mp)):
        for o in range(1, n):
            pl.semaphore_signal(
                barrier,
                inc=1,
                device_id={axis: lax.rem(me + o, n)},
                device_id_type=pl.DeviceIdType.MESH,
            )
    length = length_ref[...]
    whole_row = lax.div(length, jnp.int32(page_len))
    lines = jnp.concatenate([table_ref[...], whole_row, length - whole_row * page_len], axis=0)
    down = lax.broadcasted_iota(jnp.int32, (games, games), 0)
    across = lax.broadcasted_iota(jnp.int32, (games, games), 1)
    unit = jnp.where(down == across, 1.0, 0.0).astype(BF16)
    table = lax.dot_general(
        unit,
        lines.astype(F32).astype(BF16),
        (((1,), (1,)), ((), ())),
        preferred_element_type=F32,
    ).astype(jnp.int32)
    whole_pages = table[:, table_len : table_len + 1]
    rest = table[:, table_len + 1 : table_len + 2]
    lane = lax.broadcasted_iota(jnp.int32, (games, every), 1)
    full = jnp.zeros((games, every), F32)
    last = jnp.full((games, 1), -1, jnp.int32)
    for j in range(table_len):
        named = table[:, j : j + 1]
        full = full + jnp.where((lane == named) & (whole_pages > j), 1.0, 0.0)
        last = jnp.where(whole_pages == j, named, last)
    full = jnp.concatenate([full] * heads, axis=0)
    last = jnp.concatenate([last] * heads, axis=0)
    rest = jnp.concatenate([rest] * heads, axis=0)
    place = lax.broadcasted_iota(jnp.int32, (rows, page_len), 1)
    in_last = jnp.where(place < rest, 1.0, 0.0)

    factor = 1.0 / math.sqrt(head_size)
    query = jnp.concatenate([query_ref[:, h, :] for h in range(heads)], axis=0)
    entry = entry_ref[...].astype(F32)
    entry = jnp.concatenate([entry] * heads, axis=0)
    biggest = (
        jnp.sum(query.astype(F32) * entry[:, :head_size], axis=-1, keepdims=True) * factor
    )
    total = jnp.ones((rows, 1), F32)
    acc = entry[:, head_size:]

    for copy in pool_loads:
        copy.wait()
    pl.semaphore_wait(barrier, n_dp - 1 + n_mp - 1)

    def picked(d, c):
        page = pages[slot_ref[c, d]]
        live = jnp.full(page.shape, c < count_ref[0, d])
        return jnp.where(live, page, jnp.zeros_like(page))

    sends = []
    for o in range(n_dp - 1, 0, -1):
        to = xor(dp, o)
        for c in range(cap):
            outgoing[to * cap + c] = picked(to, c)
        copy = remote(
            outgoing.at[pl.ds(to * cap, cap)],
            landed.at[pl.ds(dp * cap, cap)],
            page_send.at[o - 1],
            page_recv.at[o - 1],
            "dp",
            to,
        )
        copy.start()
        sends.append(copy)
    for c in range(cap):
        landed[dp * cap + c] = picked(dp, c)
    weight_loads = []
    for i, (src, dst) in enumerate(((wo_hbm, wo), (wg_hbm, wg), (wu_hbm, wu), (wd_hbm, wd))):
        copy = pltpu.make_async_copy(src, dst, weight_sem.at[i])
        copy.start()
        weight_loads.append(copy)

    def attend(at, state):
        biggest, total, acc = state
        block = pages.at[pl.ds(at, group)] if at < pool else landed.at[pl.ds(at - pool, group)]
        keys = block[:, :, :head_size].reshape(group * page_len, head_size)
        values = block[:, :, head_size:].reshape(group * page_len, head_size)
        scores = (
            lax.dot_general(query, keys, (((1,), (1,)), ((), ())), preferred_element_type=F32)
            * factor
        )
        times = jnp.concatenate(
            [
                full[:, e : e + 1] + jnp.where(last == e, in_last, 0.0)
                for e in range(at, at + group)
            ],
            axis=1,
        )
        scores = jnp.where(times > 0.0, scores, -1e30)
        new = jnp.maximum(biggest, jnp.max(scores, axis=-1, keepdims=True))
        probs = times * jnp.exp(scores - new)
        shrink = jnp.exp(biggest - new)
        total = total * shrink + jnp.sum(probs, axis=-1, keepdims=True)
        acc = acc * shrink + dot(probs.astype(BF16), values)
        return new, total, acc

    state = (biggest, total, acc)
    for at in range(0, pool, group):
        state = attend(at, state)
    for o in range(1, n_dp):
        source = xor(dp, o)
        slot = landed.at[pl.ds(source * cap, cap)]
        remote(slot, slot, page_send.at[o - 1], page_recv.at[o - 1], "dp", source).wait_recv()
    arrived_copy = pltpu.make_async_copy(landed, arrived_hbm, arrived_sem)
    arrived_copy.start()
    for at in range(pool, every, group):
        state = attend(at, state)
    biggest, total, acc = state
    attended = (acc / total).astype(BF16)
    attended = jnp.concatenate(
        [attended[h * games : (h + 1) * games] for h in range(heads)], axis=1
    )
    weight_loads[0].wait()
    head = dot(attended, wo[...])
    head32[...] = head
    head16[...] = head.astype(BF16)

    def sum_mp(block, landing, base):
        for o in range(1, n_mp):
            to = lax.rem(mp + o, n_mp)
            copy = remote(
                block.at[pl.ds(pl.multiple_of(to * share, share), share)],
                landing.at[o - 1],
                z_send.at[base + o - 1],
                z_recv.at[base + o - 1],
                "mp",
                to,
            )
            copy.start()
            sends.append(copy)
        total = head32[pl.ds(pl.multiple_of(mp * share, share), share)]
        for o in range(1, n_mp):
            remote(
                landing.at[o - 1],
                landing.at[o - 1],
                z_send.at[base + o - 1],
                z_recv.at[base + o - 1],
                "mp",
                lax.rem(mp - o + n_mp, n_mp),
            ).wait_recv()
            total = total + landing[o - 1].astype(F32)
        return total

    def spread_mp(views, base):
        per = len(views(mp))
        for o in range(1, n_mp):
            for i, view in enumerate(views(mp)):
                sem = base + (o - 1) * per + i
                copy = remote(
                    view, view, z_send.at[sem], z_recv.at[sem], "mp", lax.rem(mp + o, n_mp)
                )
                copy.start()
                sends.append(copy)
        for o in range(1, n_mp):
            source = lax.rem(mp - o + n_mp, n_mp)
            for i, view in enumerate(views(source)):
                sem = base + (o - 1) * per + i
                remote(view, view, z_send.at[sem], z_recv.at[sem], "mp", source).wait_recv()

    def place_of(block):
        return (block % 2) * (n_dp // 2) + block // 2

    def own_rows(m):
        return pl.ds(pl.multiple_of(m * share, share), share)

    peers = n_mp - 1
    mine = residual_ref[own_rows(mp)].astype(F32) + sum_mp(head16, head_got, 0)
    scale = lax.rsqrt(jnp.mean(mine * mine, axis=-1, keepdims=True) + 1e-6)
    normed = (mine * scale * (1.0 + gain_ref[...])).astype(BF16)
    for k in range(2):
        feats[k, place_of(dp), own_rows(mp)] = normed[:, k * half : (k + 1) * half]
    spread_mp(lambda m: [feats.at[k, place_of(dp), own_rows(m)] for k in range(2)], peers)

    orders = [list(range(1, bits)) + [0], list(range(2, bits)) + [1, 0] if bits > 1 else [0]]
    for t in range(bits):
        waits = []
        for k in range(2):
            bit = orders[k][t]
            peer = flip(dp, bit)
            held = flips(dp, orders[k][:t])
            for i, block in enumerate(held):
                sem = (1 << t) - 1 + i
                copy = remote(
                    feats.at[k, place_of(block)],
                    feats.at[k, place_of(block)],
                    ag_send.at[k, sem],
                    ag_recv.at[k, sem],
                    "dp",
                    peer,
                )
                copy.start()
                sends.append(copy)
                other = flip(block, bit)
                waits.append(
                    remote(
                        feats.at[k, place_of(other)],
                        feats.at[k, place_of(other)],
                        ag_send.at[k, sem],
                        ag_recv.at[k, sem],
                        "dp",
                        peer,
                    )
                )
        if t < bits - 1:
            for wait in waits:
                wait.wait_recv()

    near = dp % 2
    blocks = n_dp // 2
    some_games = blocks * games
    units = wg.shape[1]
    tile = math.gcd(units, 256)

    def rows_of(side):
        return pl.ds(pl.multiple_of(side * some_games, some_games), some_games)

    def expand(side):
        @pl.loop(0, units // tile)
        def _(i):
            columns = pl.ds(pl.multiple_of(i * tile, tile), tile)
            low = feats[0, pl.ds(side * blocks, blocks)].reshape(some_games, half)
            high = feats[1, pl.ds(side * blocks, blocks)].reshape(some_games, half)
            gate = dot(low, wg[:half, columns]) + dot(high, wg[half:, columns])
            up = dot(low, wu[:half, columns]) + dot(high, wu[half:, columns])
            bent = jnp.tanh(math.sqrt(2.0 / math.pi) * (gate + 0.044715 * (gate * gate * gate)))
            hidden[rows_of(side), columns] = (0.5 * gate * (1.0 + bent) * up).astype(BF16)

    for copy in weight_loads[1:]:
        copy.wait()
    expand(near)
    for wait in waits:
        wait.wait_recv()
    expand(1 - near)

    def halving(k, t):
        order = orders[k][::-1]
        bit, after = order[t], order[t + 1 :]
        base = sum(1 << (bits - 1 - s) for s in range(t))
        peer = flip(dp, bit)
        waits = []
        for i in range(1 << len(after)):
            keep = with_bits(dp, after, i)
            copy = remote(
                part.at[k, place_of(flip(keep, bit))],
                got.at[k, base + i],
                rs_send.at[k, base + i],
                rs_recv.at[k, base + i],
                "dp",
                peer,
            )
            copy.start()
            sends.append(copy)
            waits.append((copy, keep, base + i))
        return waits

    out_tile = math.gcd(half, 512)

    def project(side, k):
        @pl.loop(0, half // out_tile)
        def _(i):
            columns = pl.ds(pl.multiple_of(k * half + i * out_tile, out_tile), out_tile)
            inner = pl.ds(pl.multiple_of(i * out_tile, out_tile), out_tile)
            block = dot(hidden[rows_of(side)], wd[:, columns]).astype(BF16)
            part[k, pl.ds(side * blocks, blocks), :, inner] = block.reshape(blocks, games, out_tile)

    waiting = []
    for k in range(2):
        project(1 - near, k)
        waiting.append(halving(k, 0))
    for k in range(2):
        project(near, k)
    for t in range(bits):
        later = []
        for k in range(2):
            for copy, keep, slot in waiting[k]:
                copy.wait_recv()
                added = part[k, place_of(keep)].astype(F32) + got[k, slot].astype(F32)
                if t == bits - 1:
                    head32[:, k * half : (k + 1) * half] = added
                    sums16[:, k * half : (k + 1) * half] = added.astype(BF16)
                else:
                    part[k, place_of(keep)] = added.astype(BF16)
            if t < bits - 1:
                later.append(halving(k, t + 1))
        waiting = later

    mixed = sum_mp(sums16, sums_got, 3 * peers)
    out_ref[own_rows(mp)] = (mine + mixed).astype(BF16)
    spread_mp(lambda m: [out_ref.at[own_rows(m)]], 4 * peers)
    for copy in sends:
        copy.wait_send()
    arrived_copy.wait()


def local(
    page_pool,
    move_count,
    send_slots,
    page_table,
    history_len,
    queries,
    new_entry,
    residual,
    out_proj,
    ffn_gain,
    gate_proj,
    up_proj,
    down_proj,
):
    n_dp = lax.axis_size("dp")
    n_mp = lax.axis_size("mp")
    pool, page_len, width = page_pool.shape
    cap = send_slots.shape[1]
    games, heads, head_size = queries.shape
    model = residual.shape[1]
    units = gate_proj.shape[1]
    half = model // 2
    share = games // n_mp
    group = math.gcd(pool, n_dp * cap, 8)
    vmem = pl.BlockSpec(memory_space=pltpu.VMEM)
    smem = pl.BlockSpec(memory_space=pltpu.SMEM)
    hbm = pl.BlockSpec(memory_space=pl.ANY)
    dma = pltpu.SemaphoreType.DMA
    z_count = 5 * (n_mp - 1)
    return pl.pallas_call(
        functools.partial(step, n_dp, n_mp),
        out_shape=(
            jax.ShapeDtypeStruct((n_dp * cap, page_len, width), BF16),
            jax.ShapeDtypeStruct((games, model), BF16),
        ),
        in_specs=[smem, smem] + [vmem] * 6 + [hbm] * 5,
        out_specs=(hbm, vmem),
        scratch_shapes=[
            pltpu.VMEM((pool, page_len, width), BF16),
            pltpu.VMEM((n_dp * cap, page_len, width), BF16),
            pltpu.VMEM((n_dp * cap, page_len, width), BF16),
            pltpu.VMEM(out_proj.shape, BF16),
            pltpu.VMEM(gate_proj.shape, BF16),
            pltpu.VMEM(up_proj.shape, BF16),
            pltpu.VMEM(down_proj.shape, BF16),
            pltpu.VMEM((games, model), F32),
            pltpu.VMEM((games, model), BF16),
            pltpu.VMEM((games, model), BF16),
            pltpu.VMEM((n_mp - 1, share, model), BF16),
            pltpu.VMEM((n_mp - 1, share, model), BF16),
            pltpu.VMEM((2, n_dp, games, half), BF16),
            pltpu.VMEM((n_dp * games, units), BF16),
            pltpu.VMEM((2, n_dp, games, half), BF16),
            pltpu.VMEM((2, n_dp - 1, games, half), BF16),
            dma((pool // group,)),
            dma((4,)),
            dma,
            dma((n_dp - 1,)),
            dma((n_dp - 1,)),
            dma((z_count,)),
            dma((z_count,)),
            dma((2, n_dp - 1)),
            dma((2, n_dp - 1)),
            dma((2, n_dp - 1)),
            dma((2, n_dp - 1)),
        ],
        compiler_params=pltpu.CompilerParams(
            collective_id=0, has_side_effects=True, vmem_limit_bytes=63 * 1024 * 1024
        ),
        cost_estimate=pl.CostEstimate(
            flops=6 * n_dp * games * model * units,
            bytes_accessed=2 * (page_pool.size + 4 * model * units),
            transcendentals=n_dp * games * units,
        ),
    )(
        move_count,
        send_slots.T,
        page_table.T,
        history_len.reshape(1, games),
        queries,
        new_entry,
        residual,
        ffn_gain.reshape(1, model),
        page_pool,
        out_proj,
        gate_proj,
        up_proj,
        down_proj,
    )


def solution(mesh):
    in_specs = (
        P("dp", None, None),
        P("dp", None),
        P("dp", None),
        P("dp", None),
        P("dp"),
        P("dp", "mp", None),
        P("dp", None),
        P("dp", None),
        P("mp", None),
        P(),
        P(None, ("dp", "mp")),
        P(None, ("dp", "mp")),
        P(("dp", "mp"), None),
    )
    out_specs = (P("dp", None, None), P("dp", None))
    return jax.shard_map(local, mesh=mesh, in_specs=in_specs, out_specs=out_specs, check_vma=False)
```
